32 devices in a mesh: gx: 8 (over z, x), gy: 4 (over y, core).
Axes of the slice: x: 2, y: 2, z: 4, core: 2. Of those that a mesh axis runs over, the one named last changes fastest.
Arguments:
- profiles: float32 [2, 32768, 128], P(None, ('gx', 'gy')), may hold values from 0.5 to 2
- radial: float32 [2, 128, 128], replicated, may hold values from -1 to 2
- rate_const: float32 [32768], P(('gx', 'gy')), may hold values from 0.02 to 0.2
- transfer_coef: float32 [32768], P(('gx', 'gy')), may hold values from 0.1 to 0.5
- live_count: int32 [32], P(('gx', 'gy')), may hold values from 256 to 1024, as said below
- send_lists: int32 [256, 128], P(('gx', 'gy')), may hold values from 0 to 1023, as said below
- cell_index: int32 [32768], P(('gx', 'gy')), may hold values from 0 to 131071
- contact_cols: int32 [256, 4], P(('gx', 'gy')), may hold values from 0 to 15, as said below
- contact_blocks: float32 [256, 4, 128, 128], P(('gx', 'gy')), may hold values from 0 to 0.006
- populations: float32 [7, 256, 128, 128], P(None, 'gx', 'gy'), may hold values from -1.8 to 1.8
Outputs:
- profiles_out: float32 [2, 32768, 128], P(None, ('gx', 'gy'))
- populations_out: float32 [7, 256, 128, 128], P(None, 'gx', 'gy')
The draws below stay inside these ranges and needn't reach their ends.
Inputs may be any that keep to these rules, and one draw needn't show every extreme that they name: `live_count`: each tile's count is a multiple of 128, at least a quarter of its slots, and some tile is full. `send_lists`: every entry names a live slot of the sending tile. `contact_cols`: blocks 0 to 7 are the tile's own, block 8 + n is ghost block n; every ghost block is named by some row block.
All inputs are finite; a program needn't handle non-finite values.
Results may differ from the reference program's by a relative error of at most 0.0001.
Values sent between devices are 32-bit elements; how exact they have to be, the bound alone decides.
A program may use at most 128 MiB of HBM per device.

```python
import math
import jax
import jax.numpy as jnp
import numpy as np
from jax import lax

NR = 128
BLK = 128
SHELL = 16
KB = 4
STEPS = 3
PBLK = 8
CX = 32
CY = 32
NZ = 128
PELLETS = 32768
NX = 256
NY = 128
N_GX = 8
N_GY = 4


def live_helper(key):
    devices = N_GX * N_GY
    blocks = jax.random.randint(jax.random.fold_in(key, 11), (devices,), max(1, PBLK // 4), PBLK + 1)
    chosen_device = jax.random.randint(jax.random.fold_in(key, 12), (), 0, devices)
    counts = jnp.where(jnp.arange(devices) == chosen_device, PBLK, blocks) * BLK
    return counts.astype(jnp.int32)


def draw_live_count(key, part):
    return live_helper(key)


def draw_send_lists(key, part):
    devices = N_GX * N_GY
    counts = live_helper(key)
    entries = jax.random.randint(jax.random.fold_in(key, 13), (devices, 8, BLK), 0, counts[:, None, None])
    return entries.reshape(devices * 8, BLK).astype(jnp.int32)


def draw_contact_cols(key, part):
    devices = N_GX * N_GY
    rows = jnp.arange(PBLK, dtype=jnp.int32)
    own_block = jnp.broadcast_to(rows[None, :], (devices, PBLK))
    first_ghost = jnp.broadcast_to((PBLK + 2 * rows % 8)[None, :], (devices, PBLK))
    second_ghost = jnp.broadcast_to((PBLK + (2 * rows + 1) % 8)[None, :], (devices, PBLK))
    extra_block = jax.random.randint(jax.random.fold_in(key, 21), (devices, PBLK), 0, PBLK + 8)
    stacked = jnp.stack([own_block, first_ghost, second_ghost, extra_block], axis=2)
    return stacked.reshape(devices * PBLK, 4).astype(jnp.int32)


def draw_radial(key, part):
    diag_key = jax.random.fold_in(key, 31)
    off_key = jax.random.fold_in(key, 32)
    diagonal_part = jax.random.uniform(diag_key, (2, NR), minval=0.55, maxval=0.95)
    spread = jnp.clip(jax.random.normal(off_key, (2, NR, NR)), -4.0, 4.0) * (0.3 / math.sqrt(NR))
    return (spread + jnp.eye(NR, dtype=jnp.float32)[None] * diagonal_part[:, :, None]).astype(jnp.float32)


def set_ends(values, stream_key, least, largest):
    spot = [jax.random.randint(jax.random.fold_in(stream_key, axis), (), 0, length) for axis, length in enumerate(values.shape)]
    widest = values.shape.index(max(values.shape))
    neighbour = spot[:widest] + [(spot[widest] + 1) % values.shape[widest]] + spot[widest + 1:]
    return values.at[tuple(spot)].set(least).at[tuple(neighbour)].set(largest)


def shard_levels(rng, shape, pieces, least, largest):
    def one(position, blocks):
        steps = jax.random.uniform(jax.random.fold_in(jax.random.fold_in(rng, 6), position), (blocks,), jnp.float32, least / len(pieces), largest / len(pieces))
        return jnp.repeat(jnp.exp(steps), shape[position] // blocks).reshape((-1,) + (1,) * (len(shape) - position - 1))

    factor_of = one(*pieces[0])
    for cut in pieces[1:]:
        factor_of = factor_of * one(*cut)
    return factor_of


def noise(stream_key, dims, scale, limit, pieces=(), kind=jnp.bfloat16):
    values = jax.random.normal(stream_key, dims, jnp.float32) * scale
    if len(pieces) > 0:
        values = shard_levels(stream_key, dims, pieces, -0.22, 0.18) * values
    return jnp.clip(values, min=-limit, max=limit).astype(kind)


def setup_inputs(seed: int = 0) -> dict:
    keys = jax.random.split(jax.random.key(seed), 11)
    profiles = jnp.clip(0.5 + 1.5 * jax.random.uniform(keys[0], (2, PELLETS, NR), jnp.float32) ** shard_levels(keys[0], (2, PELLETS, NR), ((1, 32),), -0.2, 0.2), 0.5, 2.0)
    radial = draw_radial(jax.random.fold_in(keys[10], 71), 0)
    rate_const = jnp.clip(jnp.exp(math.log(0.2) - 2.3025851 * jax.random.uniform(keys[2], (PELLETS,), jnp.float32) ** shard_levels(keys[2], (PELLETS,), ((0, 32),), -0.2, 0.2)), 0.02, 0.2)
    transfer_coef = jnp.clip(jnp.exp(math.log(0.5) - 1.609438 * jax.random.uniform(keys[3], (PELLETS,), jnp.float32) ** shard_levels(keys[3], (PELLETS,), ((0, 32),), -0.2, 0.2)), 0.1, 0.5)
    live_count = draw_live_count(jax.random.fold_in(keys[10], 71), 0)
    send_lists = draw_send_lists(jax.random.fold_in(keys[10], 71), 0)
    cell_index = set_ends(jax.random.randint(keys[6], (PELLETS,), 0, CX * CY * NZ), jax.random.fold_in(keys[6], 1), 0, (CX * CY * NZ) - 1).astype(jnp.int32)
    contact_cols = draw_contact_cols(jax.random.fold_in(keys[10], 71), 0)
    contact_blocks = jnp.clip(0.006 * jax.random.uniform(keys[8], (N_GX * N_GY * PBLK, KB, BLK, BLK), jnp.float32) ** shard_levels(keys[8], (N_GX * N_GY * PBLK, KB, BLK, BLK), ((0, 32),), -0.2, 0.2), 0.0, 0.006)
    populations = noise(keys[9], (7, NX, NY, NZ), 0.3, 1.8, ((1, 8), (2, 4)), jnp.float32)
    return dict(profiles=profiles, radial=radial, rate_const=rate_const, transfer_coef=transfer_coef, live_count=live_count, send_lists=send_lists, cell_index=cell_index, contact_cols=contact_cols, contact_blocks=contact_blocks, populations=populations)


OFFSETS = ((-1, -1), (-1, 0), (-1, 1), (0, -1), (0, 1), (1, -1), (1, 0), (1, 1))
LATTICE_WEIGHTS = np.array([0.25, 0.125, 0.125, 0.125, 0.125, 0.125, 0.125], dtype=np.float32)


def shift_axis(values, amount, axis_number):
    if amount == 0:
        return values
    length = values.shape[axis_number]
    zeros_part = jnp.zeros_like(lax.slice_in_dim(values, 0, 1, axis=axis_number))
    if amount == 1:
        return jnp.concatenate([zeros_part, lax.slice_in_dim(values, 0, length - 1, axis=axis_number)], axis=axis_number)
    return jnp.concatenate([lax.slice_in_dim(values, 1, length, axis=axis_number), zeros_part], axis=axis_number)


def shift_grid(values, offset_x, offset_y):
    return shift_axis(shift_axis(values, offset_x, 0), offset_y, 1)


def stream_cells(post):
    padded = jnp.pad(post, ((0, 0), (1, 1), (1, 1), (1, 1)))
    return jnp.stack([
        padded[0, 1:-1, 1:-1, 1:-1],
        padded[1, :-2, 1:-1, 1:-1],
        padded[2, 2:, 1:-1, 1:-1],
        padded[3, 1:-1, :-2, 1:-1],
        padded[4, 1:-1, 2:, 1:-1],
        padded[5, 1:-1, 1:-1, :-2],
        padded[6, 1:-1, 1:-1, 2:],
    ])


def reference(profiles, radial, rate_const, transfer_coef, live_count, send_lists, cell_index, contact_cols, contact_blocks, populations):
    slots = PBLK * BLK
    tiles_x = N_GX
    tiles_y = N_GY
    total = slots * tiles_x * tiles_y
    weights = jnp.asarray(LATTICE_WEIGHTS).reshape(7, 1, 1, 1)
    live = (jnp.arange(slots, dtype=jnp.int32)[None, :] < live_count[:, None]).astype(jnp.float32).reshape(-1)
    ones_grid = jnp.ones((tiles_x, tiles_y), jnp.float32)
    exists = jnp.stack([shift_grid(ones_grid, pair[0], pair[1]) for pair in OFFSETS], axis=2)
    ghost_live = jnp.broadcast_to(exists[:, :, :, None], (tiles_x, tiles_y, 8, BLK)).reshape(tiles_x, tiles_y, 8 * BLK)
    live_ext = jnp.concatenate([live.reshape(tiles_x, tiles_y, slots), ghost_live], axis=2).reshape(tiles_x, tiles_y, PBLK + 8, BLK)
    lists = send_lists.reshape(tiles_x, tiles_y, 8, BLK)
    columns = contact_cols.reshape(tiles_x, tiles_y, PBLK, KB)
    blocks = contact_blocks.reshape(tiles_x, tiles_y, PBLK, KB, BLK, BLK)
    picker = jax.vmap(jax.vmap(lambda table, where_rows: table[where_rows]))
    tile_of = jnp.arange(total, dtype=jnp.int32) // slots
    tile_row = tile_of // tiles_y
    tile_col = tile_of % tiles_y
    local_x = cell_index // (CY * NZ)
    local_y = (cell_index // NZ) % CY
    local_z = cell_index % NZ
    global_cell = ((tile_row * CX + local_x) * (CY * tiles_y) + tile_col * CY + local_y) * NZ + local_z
    picked_live = picker(live_ext, columns)
    for turn_index in range(STEPS):
        temp = profiles[0]
        conc = profiles[1]
        theta = jnp.sum(populations, axis=0)
        shell = temp[:, NR - SHELL:]
        buffers = picker(shell.reshape(tiles_x, tiles_y, slots, SHELL), lists)
        ghosts = jnp.stack([shift_grid(buffers[:, :, number], OFFSETS[number][0], OFFSETS[number][1]) for number in range(8)], axis=2)
        own_rows = (shell * live[:, None]).reshape(tiles_x, tiles_y, slots, SHELL)
        extended = jnp.concatenate([own_rows, ghosts.reshape(tiles_x, tiles_y, 8 * BLK, SHELL)], axis=2).reshape(tiles_x, tiles_y, PBLK + 8, BLK, SHELL)
        picked = picker(extended, columns)
        flow = jnp.einsum("xyrkab,xyrkbs->xyras", blocks, picked, precision=lax.Precision.HIGHEST).reshape(total, SHELL)
        sink = jnp.einsum("xyrkab,xyrkb->xyra", blocks, picked_live, precision=lax.Precision.HIGHEST).reshape(total)
        contact = flow - sink[:, None] * shell
        theta_cell = theta.reshape(-1)[global_cell]
        exchange = transfer_coef * (theta_cell - temp[:, NR - 1]) * live
        rate = rate_const[:, None] * conc * jnp.exp(0.5 * jnp.tanh(temp - 1.0))
        mixed = jnp.einsum("cpj,cjk->cpk", profiles, radial, precision=lax.Precision.HIGHEST)
        new_temp = mixed[0] + rate
        new_temp = new_temp.at[:, NR - SHELL:].add(contact)
        new_temp = new_temp.at[:, NR - 1].add(exchange)
        new_conc = mixed[1] - rate
        updated = jnp.stack([new_temp, new_conc])
        profiles = jnp.where(live[None, :, None] > 0.0, updated, profiles)
        source = -0.5 * jax.ops.segment_sum(exchange, global_cell, num_segments=theta.size).reshape(theta.shape)
        post = populations - (populations - weights * theta[None]) / 0.8 + weights * source[None]
        populations = stream_cells(post)
    return profiles, populations
```

```python
import jax
import jax.numpy as jnp
import numpy as np
from jax import lax
from jax.experimental import pallas as pl
from jax.experimental.pallas import tpu as pltpu
from jax.sharding import PartitionSpec as P

BLK = 128
SHELL = 16
STEPS = 3
OFFSETS = ((-1, -1), (-1, 0), (-1, 1), (0, -1), (0, 1), (1, -1), (1, 0), (1, 1))
SIDES = ((1, 0), (-1, 0), (0, 1), (0, -1))
MESH = pl.DeviceIdType.MESH
F32 = jnp.float32
BF16 = jnp.bfloat16


def high_part(value):
    return value.astype(BF16).astype(F32)


def dot(a, b):
    return jnp.dot(a, b, preferred_element_type=F32)


def roll(value, amount, axis):
    amount = amount % value.shape[axis]
    return value if amount == 0 else pltpu.roll(value, amount, axis)


def kernel(
    live_ref, cols_ref, rate_ref, coef_ref, cell_ref, lists_ref, radial_ref,
    prof_in, blocks_in, pop_in,
    prof_out, pop_out,
    prof, pop, raw, blocks, mixer, pick, pick_t, listed, zmask, coef, rate_c,
    shells, ext, theta, theta_s, cell_ex, ex_s, q_ref,
    send_g, recv_g, send_h, recv_h,
    in_sems, out_sems, gs_sems, gr_sems, hs_sems, hr_sems,
):
    own = prof.shape[1] // BLK
    cx, cy, nz = theta.shape
    rows = cx * cy
    kb = cols_ref.shape[1]
    ix, iy = lax.axis_index("gx"), lax.axis_index("gy")
    sx, sy = lax.axis_size("gx"), lax.axis_size("gy")

    def there(ox, oy):
        x, y = ix + ox, iy + oy
        return (x >= 0) & (x < sx) & (y >= 0) & (y < sy)

    load_prof = pltpu.make_async_copy(prof_in, prof, in_sems.at[0])
    load_pop = pltpu.make_async_copy(pop_in, pop.at[0, :, pl.ds(1, cx)], in_sems.at[1])
    load_blocks = pltpu.make_async_copy(blocks_in, raw, in_sems.at[2])
    load_prof.start()
    load_pop.start()
    load_blocks.start()

    recv_g[...] = jnp.zeros_like(recv_g)
    recv_h[...] = jnp.zeros_like(recv_h)
    barrier = pltpu.get_barrier_semaphore()
    for ox, oy in OFFSETS:
        @pl.when(there(ox, oy))
        def _():
            pl.semaphore_signal(barrier, inc=1, device_id=(ix + ox, iy + oy), device_id_type=MESH)

    live_count = live_ref[0]
    sub = lax.broadcasted_iota(jnp.int32, (BLK, BLK), 0)
    lane = lax.broadcasted_iota(jnp.int32, (BLK, BLK), 1)
    lane_f = lane.astype(F32)
    sub_f = sub.astype(F32)
    in_shell = lane >= BLK - SHELL
    in_live = (lane >= BLK - 3 * SHELL) & (lane < BLK - 2 * SHELL)

    def one_hot(match):
        return jnp.where(match, 1.0, 0.0).astype(BF16)

    def column(row):
        return jnp.broadcast_to(row, (BLK, BLK)).T

    def setup(c, carry):
        span = pl.ds(pl.multiple_of(c * BLK, BLK), BLK)
        at = pl.ds(c, 1)
        cell = cell_ref[at, :]
        row_col = column((cell // nz).astype(F32))
        z_col = column((cell % nz).astype(F32))
        list_col = column(lists_ref[at, :].astype(F32))
        zmask[span, :] = jnp.where(z_col == lane_f, 1.0, 0.0)
        coef[span, :] = jnp.where(sub + c * BLK < live_count, column(coef_ref[at, :]), 0.0)
        rate_c[span, :] = column(rate_ref[at, :])
        for d in range(rows // BLK):
            pick[span, d * BLK:(d + 1) * BLK] = one_hot(row_col == lane_f + d * BLK)
        for d in range(own):
            listed[span, d * BLK:(d + 1) * BLK] = one_hot(list_col == lane_f + d * BLK)
        return carry

    lax.fori_loop(0, own, setup, 0)

    def setup_t(c, carry):
        span = pl.ds(pl.multiple_of(c * BLK, BLK), BLK)
        base = sub_f + (c * BLK).astype(F32)
        for d in range(own):
            row = (cell_ref[d:d + 1, :] // nz).astype(F32)
            pick_t[span, d * BLK:(d + 1) * BLK] = one_hot(jnp.broadcast_to(row, (BLK, BLK)) == base)
        return carry

    lax.fori_loop(0, rows // BLK, setup_t, 0)

    for c in range(2):
        value = radial_ref[c]
        high = value.astype(BF16)
        low = (value - high.astype(F32)).astype(BF16)
        mixer[c, :BLK, :BLK] = high
        mixer[c, :BLK, BLK:] = low
        mixer[c, BLK:, :BLK] = high
        mixer[c, BLK:, BLK:] = jnp.zeros_like(high)

    load_blocks.wait()

    def split_block(i, carry):
        value = raw[i]
        high = value.astype(BF16)
        blocks[i, :, :BLK] = high
        blocks[i, :, BLK:] = (value - high.astype(F32)).astype(BF16)
        return carry

    lax.fori_loop(0, own * kb, split_block, 0)
    load_prof.wait()
    load_pop.wait()
    count_x = 1 + (ix > 0).astype(jnp.int32) + (ix < sx - 1).astype(jnp.int32)
    count_y = 1 + (iy > 0).astype(jnp.int32) + (iy < sy - 1).astype(jnp.int32)
    pl.semaphore_wait(barrier, count_x * count_y - 1)

    def ghost_copy(step, n):
        ox, oy = OFFSETS[n]
        return pltpu.make_async_remote_copy(
            src_ref=send_g.at[step, n], dst_ref=recv_g.at[step, n],
            send_sem=gs_sems.at[step, n], recv_sem=gr_sems.at[step, n],
            device_id=(ix + ox, iy + oy), device_id_type=MESH)

    def halo_copy(step, n):
        ox, oy = SIDES[n]
        return pltpu.make_async_remote_copy(
            src_ref=send_h.at[step, n], dst_ref=recv_h.at[step, n],
            send_sem=hs_sems.at[step, n], recv_sem=hr_sems.at[step, n],
            device_id=(ix + ox, iy + oy), device_id_type=MESH)

    def one_step(step, carry):
        cur = lax.rem(step, 2)
        nxt = 1 - cur

        def prepare(r, carry):
            span = pl.ds(pl.multiple_of(r * BLK, BLK), BLK)
            value = jnp.where(in_shell, prof[0, span, :], 0.0)
            high = high_part(value)
            low = value - high
            mid = high_part(low)
            low_rolled = roll(low, -SHELL, 1)
            shells[span, :] = (high + roll(mid, -SHELL, 1) + roll(low - mid, -2 * SHELL, 1)).astype(BF16)
            live = sub + r * BLK < live_count
            marked = high + jnp.where(in_live, 1.0, 0.0)
            ext[r, :BLK, :] = jnp.where(live, marked + low_rolled, 0.0).astype(BF16)
            ext[r, BLK:, :] = jnp.where(live, marked, 0.0).astype(BF16)
            return carry

        lax.fori_loop(0, own, prepare, 0)

        def gather_ghosts(n, carry):
            span = pl.ds(pl.multiple_of(n * BLK, BLK), BLK)
            found = dot(listed[span, :], shells[...])
            found = found + roll(found, SHELL, 1) + roll(found, 2 * SHELL, 1)
            found = jnp.where(in_shell, found, 0.0)
            packed = jnp.zeros((SHELL, BLK), F32)
            for j in range(BLK // SHELL):
                packed = packed + roll(found[j * SHELL:(j + 1) * SHELL, :], (j + 1) * SHELL, 1)
            send_g[step, n] = packed
            return carry

        lax.fori_loop(0, 8, gather_ghosts, 0)
        for n in range(8):
            @pl.when(there(*OFFSETS[n]))
            def _():
                ghost_copy(step, n).start()

        def sum_theta(x, carry):
            total = pop[cur, 0, x + 1]
            for i in range(1, 7):
                total = total + pop[cur, i, x + 1]
            theta[x] = total
            span = pl.ds(pl.multiple_of(x * cy, cy), cy)
            high = total.astype(BF16)
            theta_s[span, :nz] = high
            theta_s[span, nz:] = (total - high.astype(F32)).astype(BF16)
            return carry

        lax.fori_loop(0, cx, sum_theta, 0)
        ones = jnp.ones((2 * nz, BLK), BF16)

        def gather_theta(c, carry):
            span = pl.ds(pl.multiple_of(c * 2 * BLK, 2 * BLK), 2 * BLK)
            found = dot(pick[span, :], theta_s[...])
            mask = zmask[span, :]
            kept = jnp.concatenate([found[:, :nz] * mask, found[:, nz:] * mask], axis=1).astype(BF16)
            at_cell = dot(kept, ones)
            last = jnp.broadcast_to(prof[0, span, BLK - 1:], (2 * BLK, BLK))
            value = coef[span, :] * (at_cell - last)
            cell_ex[span, :] = value
            value = value * mask
            high = value.astype(BF16)
            ex_s[span, :nz] = high
            ex_s[span, nz:] = (value - high.astype(F32)).astype(BF16)
            return carry

        lax.fori_loop(0, own // 2, gather_theta, 0)
        slabs = 2 * BLK // cy

        def scatter(c, carry):
            span = pl.ds(pl.multiple_of(c * 2 * BLK, 2 * BLK), 2 * BLK)
            found = dot(pick_t[span, :], ex_s[...])
            some = pl.ds(c * slabs, slabs)
            total = (found[:, :nz] + found[:, nz:]).reshape(slabs, cy, nz)
            q_ref[some] = 1.25 * theta[some] - 0.5 * total
            return carry

        lax.fori_loop(0, rows // (2 * BLK), scatter, 0)
        zlane = lax.broadcasted_iota(jnp.int32, (cy, nz), 1)

        def stream(x, carry):
            q = q_ref[x]
            part = 0.125 * q
            pop[nxt, 0, x + 1] = 0.25 * (q - pop[cur, 0, x + 1])
            pop[nxt, 1, x + 2] = part - 0.25 * pop[cur, 1, x + 1]
            pop[nxt, 2, x] = part - 0.25 * pop[cur, 2, x + 1]
            up = roll(part - 0.25 * pop[cur, 3, x + 1], 1, 0)
            down = roll(part - 0.25 * pop[cur, 4, x + 1], -1, 0)
            pop[nxt, 3, x + 1] = up
            pop[nxt, 4, x + 1] = down
            send_h[step, 2, pl.ds(x, 1), :] = up[:1]
            send_h[step, 3, pl.ds(x, 1), :] = down[cy - 1:]
            above = roll(part - 0.25 * pop[cur, 5, x + 1], 1, 1)
            below = roll(part - 0.25 * pop[cur, 6, x + 1], -1, 1)
            pop[nxt, 5, x + 1] = jnp.where(zlane == 0, 0.0, above)
            pop[nxt, 6, x + 1] = jnp.where(zlane == nz - 1, 0.0, below)
            return carry

        lax.fori_loop(0, cx, stream, 0)
        send_h[step, 0] = pop[nxt, 1, cx + 1]
        send_h[step, 1] = pop[nxt, 2, 0]
        for n in range(4):
            @pl.when(there(*SIDES[n]))
            def _():
                halo_copy(step, n).start()

        for n in range(8):
            ox, oy = OFFSETS[n]
            here = there(-ox, -oy)

            @pl.when(here)
            def _():
                ghost_copy(step, n).wait_recv()

        shell16 = lax.broadcasted_iota(jnp.int32, (SHELL, BLK), 1)
        ghost_shell = shell16 >= BLK - SHELL
        ghost_live = (shell16 >= BLK - 3 * SHELL) & (shell16 < BLK - 2 * SHELL)
        for n in range(8):
            ox, oy = OFFSETS[n]
            mark = jnp.where(ghost_live, there(-ox, -oy).astype(F32), 0.0)
            packed = recv_g[step, n]
            for j in range(BLK // SHELL):
                value = jnp.where(ghost_shell, roll(packed, BLK - (j + 1) * SHELL, 1), 0.0)
                high = high_part(value)
                marked = high + mark
                ext[own + n, j * SHELL:(j + 1) * SHELL, :] = (marked + roll(value - high, -SHELL, 1)).astype(BF16)
                ext[own + n, BLK + j * SHELL:BLK + (j + 1) * SHELL, :] = marked.astype(BF16)

        def update(r, carry):
            span = pl.ds(pl.multiple_of(r * BLK, BLK), BLK)
            temp = prof[0, span, :]
            conc = prof[1, span, :]
            mixed = []
            for c, value in enumerate((temp, conc)):
                high = value.astype(BF16)
                low = (value - high.astype(F32)).astype(BF16)
                both = dot(jnp.concatenate([high, low], axis=1), mixer[c])
                mixed.append(both[:, :BLK] + both[:, BLK:])
            total = jnp.zeros((BLK, BLK), F32)
            for k in range(kb):
                total = total + dot(blocks[r * kb + k], ext[cols_ref[r, k]])
            contact = total + roll(total, SHELL, 1) - roll(total, 2 * SHELL, 1) * temp
            rate = rate_c[span, :] * conc * jnp.exp(0.5 * jnp.tanh(temp - 1.0))
            new_temp = mixed[0] + rate + jnp.where(in_shell, contact, 0.0)
            new_temp = new_temp + jnp.where(lane == BLK - 1, cell_ex[span, :], 0.0)
            live = sub + r * BLK < live_count
            prof[0, span, :] = jnp.where(live, new_temp, temp)
            prof[1, span, :] = jnp.where(live, mixed[1] - rate, conc)
            return carry

        lax.fori_loop(0, own, update, 0)

        for n in range(4):
            ox, oy = SIDES[n]

            @pl.when(there(-ox, -oy))
            def _():
                halo_copy(step, n).wait_recv()

        pop[nxt, 1, 1] = recv_h[step, 0]
        pop[nxt, 2, cx] = recv_h[step, 1]

        def edges(x, carry):
            pop[nxt, 3, x + 1, pl.ds(0, 1), :] = recv_h[step, 2, pl.ds(x, 1), :]
            pop[nxt, 4, x + 1, pl.ds(cy - 1, 1), :] = recv_h[step, 3, pl.ds(x, 1), :]
            return carry

        lax.fori_loop(0, cx, edges, 0)
        return carry

    lax.fori_loop(0, STEPS, one_step, 0)
    store_prof = pltpu.make_async_copy(prof, prof_out, out_sems.at[0])
    store_pop = pltpu.make_async_copy(pop.at[STEPS % 2, :, pl.ds(1, cx)], pop_out, out_sems.at[1])
    store_prof.start()
    store_pop.start()
    for step in range(STEPS):
        for n in range(8):
            @pl.when(there(*OFFSETS[n]))
            def _():
                ghost_copy(step, n).wait_send()
        for n in range(4):
            @pl.when(there(*SIDES[n]))
            def _():
                halo_copy(step, n).wait_send()
    store_prof.wait()
    store_pop.wait()


def on_device(
    profiles, radial, rate_const, transfer_coef, live_count, send_lists, cell_index, contact_cols,
    contact_blocks, populations,
):
    slots = profiles.shape[1]
    own = slots // BLK
    kb = contact_cols.shape[1]
    _, cx, cy, nz = populations.shape
    rows = cx * cy
    vmem = pl.BlockSpec(memory_space=pltpu.VMEM)
    smem = pl.BlockSpec(memory_space=pltpu.SMEM)
    anywhere = pl.BlockSpec(memory_space=pl.ANY)
    return pl.pallas_call(
        kernel,
        out_shape=(
            jax.ShapeDtypeStruct(profiles.shape, F32),
            jax.ShapeDtypeStruct(populations.shape, F32),
        ),
        in_specs=[smem, smem, vmem, vmem, vmem, vmem, vmem, anywhere, anywhere, anywhere],
        out_specs=(anywhere, anywhere),
        scratch_shapes=[
            pltpu.VMEM(profiles.shape, F32),
            pltpu.VMEM((2, 7, cx + 2, cy, nz), F32),
            pltpu.VMEM((own * kb, BLK, BLK), F32),
            pltpu.VMEM((own * kb, BLK, 2 * BLK), BF16),
            pltpu.VMEM((2, 2 * BLK, 2 * BLK), BF16),
            pltpu.VMEM((slots, rows), BF16),
            pltpu.VMEM((rows, slots), BF16),
            pltpu.VMEM((8 * BLK, slots), BF16),
            pltpu.VMEM((slots, nz), F32),
            pltpu.VMEM((slots, BLK), F32),
            pltpu.VMEM((slots, BLK), F32),
            pltpu.VMEM((slots, BLK), BF16),
            pltpu.VMEM((own + 8, 2 * BLK, BLK), BF16),
            pltpu.VMEM((cx, cy, nz), F32),
            pltpu.VMEM((rows, 2 * nz), BF16),
            pltpu.VMEM((slots, BLK), F32),
            pltpu.VMEM((slots, 2 * nz), BF16),
            pltpu.VMEM((cx, cy, nz), F32),
            pltpu.VMEM((STEPS, 8, SHELL, BLK), F32),
            pltpu.VMEM((STEPS, 8, SHELL, BLK), F32),
            pltpu.VMEM((STEPS, 4, cx, nz), F32),
            pltpu.VMEM((STEPS, 4, cx, nz), F32),
            pltpu.SemaphoreType.DMA((3,)),
            pltpu.SemaphoreType.DMA((2,)),
            pltpu.SemaphoreType.DMA((STEPS, 8)),
            pltpu.SemaphoreType.DMA((STEPS, 8)),
            pltpu.SemaphoreType.DMA((STEPS, 4)),
            pltpu.SemaphoreType.DMA((STEPS, 4)),
        ],
        compiler_params=pltpu.CompilerParams(
            collective_id=0, has_side_effects=True, vmem_limit_bytes=48 * 1024 * 1024
        ),
    )(
        live_count,
        contact_cols,
        rate_const.reshape(own, BLK),
        transfer_coef.reshape(own, BLK),
        cell_index.reshape(own, BLK),
        send_lists,
        radial,
        profiles,
        contact_blocks.reshape(own * kb, BLK, BLK),
        populations,
    )


def solution(mesh):
    return jax.shard_map(
        on_device,
        mesh=mesh,
        in_specs=(
            P(None, ("gx", "gy"), None),
            P(),
            P(("gx", "gy")),
            P(("gx", "gy")),
            P(("gx", "gy")),
            P(("gx", "gy"), None),
            P(("gx", "gy")),
            P(("gx", "gy"), None),
            P(("gx", "gy"), None, None, None),
            P(None, "gx", "gy", None),
        ),
        out_specs=(P(None, ("gx", "gy"), None), P(None, "gx", "gy", None)),
        check_vma=False,
    )
```

```python
import jax
import jax.numpy as jnp
import numpy as np
from jax import lax
from jax.experimental import pallas as pl
from jax.experimental.pallas import tpu as pltpu
from jax.sharding import PartitionSpec as P

BLK = 128
SHELL = 16
STEPS = 3
OFFSETS = ((-1, -1), (-1, 0), (-1, 1), (0, -1), (0, 1), (1, -1), (1, 0), (1, 1))
SIDES = ((1, 0), (-1, 0), (0, 1), (0, -1))
MESH = pl.DeviceIdType.MESH
F32 = jnp.float32
BF16 = jnp.bfloat16


def high_part(value):
    return value.astype(BF16).astype(F32)


def dot(a, b):
    return jnp.dot(a, b, preferred_element_type=F32)


def roll(value, amount, axis):
    amount = amount % value.shape[axis]
    return value if amount == 0 else pltpu.roll(value, amount, axis)


def kernel(
    live_ref, cols_ref, rate_in, coef_in, cell_in, lists_in, radial_in,
    prof_in, blocks_in, pop_in,
    prof, pop_b,
    pop_a, rate_ref, coef_ref, cell_ref, lists_ref, radial_ref,
    raw, blocks, mixer, pick, pick_t, listed, zmask, coef, rate_c,
    shells, ext, theta, theta_s, cell_ex, ex_s, q_ref,
    send_g, recv_g, send_h, recv_h,
    in_sems, gs_sems, gr_sems, hs_sems, hr_sems,
):
    own = prof.shape[1] // BLK
    cx, cy, nz = theta.shape
    rows = cx * cy
    kb = cols_ref.shape[0]
    ix, iy = lax.axis_index("gx"), lax.axis_index("gy")
    sx, sy = lax.axis_size("gx"), lax.axis_size("gy")

    def there(ox, oy):
        x, y = ix + ox, iy + oy
        return (x >= 0) & (x < sx) & (y >= 0) & (y < sy)

    small = [
        pltpu.make_async_copy(source, target, in_sems.at[3 + i])
        for i, (source, target) in enumerate((
            (lists_in, lists_ref), (cell_in, cell_ref), (coef_in, coef_ref), (rate_in, rate_ref),
            (radial_in, radial_ref)))
    ]
    load_prof = pltpu.make_async_copy(prof_in, prof, in_sems.at[0])
    load_pop = pltpu.make_async_copy(pop_in, pop_a.at[:, pl.ds(1, cx)], in_sems.at[1])
    load_blocks = pltpu.make_async_copy(blocks_in, raw, in_sems.at[2])
    for load in small:
        load.start()
    load_prof.start()
    load_pop.start()
    load_blocks.start()

    recv_g[...] = jnp.zeros_like(recv_g)
    recv_h[...] = jnp.zeros_like(recv_h)
    barrier = pltpu.get_barrier_semaphore()
    for ox, oy in OFFSETS:
        @pl.when(there(ox, oy))
        def _():
            pl.semaphore_signal(barrier, inc=1, device_id=(ix + ox, iy + oy), device_id_type=MESH)

    live_count = live_ref[0]
    sub = lax.broadcasted_iota(jnp.int32, (BLK, BLK), 0)
    lane = lax.broadcasted_iota(jnp.int32, (BLK, BLK), 1)
    lane_f = lane.astype(F32)
    sub_f = sub.astype(F32)
    wide_sub = lax.broadcasted_iota(jnp.int32, (2 * BLK, BLK), 0)
    wide_lane = lax.broadcasted_iota(jnp.int32, (2 * BLK, BLK), 1)
    in_shell = lane >= BLK - SHELL
    in_live = (lane >= BLK - 3 * SHELL) & (lane < BLK - 2 * SHELL)

    def one_hot(match):
        return jnp.where(match, 1.0, 0.0).astype(BF16)

    def column(row):
        return jnp.broadcast_to(row, (BLK, BLK)).T

    for load in small:
        load.wait()

    def setup(c, carry):
        span = pl.ds(pl.multiple_of(c * BLK, BLK), BLK)
        at = pl.ds(c, 1)
        cell = cell_ref[at, :]
        row_col = column((cell // nz).astype(F32))
        z_col = column((cell % nz).astype(F32))
        list_col = column(lists_ref[at, :].astype(F32))
        zmask[span, :] = jnp.where(z_col == lane_f, 1.0, 0.0)
        coef[span, :] = jnp.where(sub + c * BLK < live_count, column(coef_ref[at, :]), 0.0)
        rate_c[span, :] = column(rate_ref[at, :])
        for d in range(rows // BLK):
            pick[span, d * BLK:(d + 1) * BLK] = one_hot(row_col == lane_f + d * BLK)
        for d in range(own):
            listed[span, d * BLK:(d + 1) * BLK] = one_hot(list_col == lane_f + d * BLK)
        return carry

    lax.fori_loop(0, own, setup, 0)

    def setup_t(c, carry):
        span = pl.ds(pl.multiple_of(c * BLK, BLK), BLK)
        base = sub_f + (c * BLK).astype(F32)
        for d in range(own):
            row = (cell_ref[d:d + 1, :] // nz).astype(F32)
            pick_t[span, d * BLK:(d + 1) * BLK] = one_hot(jnp.broadcast_to(row, (BLK, BLK)) == base)
        return carry

    lax.fori_loop(0, rows // BLK, setup_t, 0)

    for c in range(2):
        value = radial_ref[c]
        high = value.astype(BF16)
        low = (value - high.astype(F32)).astype(BF16)
        mixer[c, :BLK, :BLK] = high
        mixer[c, :BLK, BLK:] = low
        mixer[c, BLK:, :BLK] = high
        mixer[c, BLK:, BLK:] = jnp.zeros_like(high)

    load_prof.wait()
    count_x = 1 + (ix > 0).astype(jnp.int32) + (ix < sx - 1).astype(jnp.int32)
    count_y = 1 + (iy > 0).astype(jnp.int32) + (iy < sy - 1).astype(jnp.int32)
    pl.semaphore_wait(barrier, count_x * count_y - 1)

    def ghost_copy(step, n):
        ox, oy = OFFSETS[n]
        return pltpu.make_async_remote_copy(
            src_ref=send_g.at[step, n], dst_ref=recv_g.at[step, n],
            send_sem=gs_sems.at[step, n], recv_sem=gr_sems.at[step, n],
            device_id=(ix + ox, iy + oy), device_id_type=MESH)

    def halo_copy(step, n):
        ox, oy = SIDES[n]
        return pltpu.make_async_remote_copy(
            src_ref=send_h.at[step, n], dst_ref=recv_h.at[step, n],
            send_sem=hs_sems.at[step, n], recv_sem=hr_sems.at[step, n],
            device_id=(ix + ox, iy + oy), device_id_type=MESH)

    def one_step(step, old, new):
        def prepare(r, carry):
            span = pl.ds(pl.multiple_of(r * BLK, BLK), BLK)
            value = jnp.where(in_shell, prof[0, span, :], 0.0)
            high = high_part(value)
            low = value - high
            mid = high_part(low)
            low_rolled = roll(low, -SHELL, 1)
            shells[span, :] = (high + roll(mid, -SHELL, 1) + roll(low - mid, -2 * SHELL, 1)).astype(BF16)
            live = sub + r * BLK < live_count
            marked = high + jnp.where(in_live, 1.0, 0.0)
            ext[r, :BLK, :] = jnp.where(live, marked + low_rolled, 0.0).astype(BF16)
            ext[r, BLK:, :] = jnp.where(live, marked, 0.0).astype(BF16)
            return carry

        lax.fori_loop(0, own, prepare, 0)

        def gather_ghosts(n, carry):
            span = pl.ds(pl.multiple_of(n * 4 * BLK, 4 * BLK), 4 * BLK)
            several = dot(listed[span, :], shells[...])
            for m in range(4):
                found = several[m * BLK:(m + 1) * BLK, :]
                found = found + roll(found, SHELL, 1) + roll(found, 2 * SHELL, 1)
                found = jnp.where(in_shell, found, 0.0)
                packed = jnp.zeros((SHELL, BLK), F32)
                for j in range(BLK // SHELL):
                    packed = packed + roll(found[j * SHELL:(j + 1) * SHELL, :], (j + 1) * SHELL, 1)
                send_g[step, n * 4 + m] = packed
            return carry

        lax.fori_loop(0, 2, gather_ghosts, 0)
        for n in range(8):
            @pl.when(there(*OFFSETS[n]))
            def _():
                ghost_copy(step, n).start()

        if step == 0:
            load_pop.wait()

        def sum_theta(c, carry):
            for u in range(4):
                x = c * 4 + u
                total = old[0, x + 1]
                for i in range(1, 7):
                    total = total + old[i, x + 1]
                theta[x] = total
                span = pl.ds(pl.multiple_of(x * cy, cy), cy)
                high = total.astype(BF16)
                theta_s[span, :nz] = high
                theta_s[span, nz:] = (total - high.astype(F32)).astype(BF16)
            return carry

        lax.fori_loop(0, cx // 4, sum_theta, 0)
        ones = jnp.ones((2 * nz, BLK), BF16)

        def gather_theta(c, carry):
            span = pl.ds(pl.multiple_of(c * 4 * BLK, 4 * BLK), 4 * BLK)
            found = dot(pick[span, :], theta_s[...])
            mask = zmask[span, :]
            kept = jnp.concatenate([found[:, :nz] * mask, found[:, nz:] * mask], axis=1).astype(BF16)
            at_cell = dot(kept, ones)
            last = jnp.broadcast_to(prof[0, span, BLK - 1:], (4 * BLK, BLK))
            value = coef[span, :] * (at_cell - last)
            cell_ex[span, :] = value
            value = value * mask
            high = value.astype(BF16)
            ex_s[span, :nz] = high
            ex_s[span, nz:] = (value - high.astype(F32)).astype(BF16)
            return carry

        lax.fori_loop(0, own // 4, gather_theta, 0)
        slabs = 4 * BLK // cy

        def scatter(c, carry):
            span = pl.ds(pl.multiple_of(c * 4 * BLK, 4 * BLK), 4 * BLK)
            found = dot(pick_t[span, :], ex_s[...])
            some = pl.ds(c * slabs, slabs)
            total = (found[:, :nz] + found[:, nz:]).reshape(slabs, cy, nz)
            q_ref[some] = 1.25 * theta[some] - 0.5 * total
            return carry

        lax.fori_loop(0, rows // (4 * BLK), scatter, 0)
        zlane = lax.broadcasted_iota(jnp.int32, (cy, nz), 1)

        def stream(c, carry):
            for u in range(2):
                x = c * 2 + u
                q = q_ref[x]
                part = 0.125 * q
                new[0, x + 1] = 0.25 * (q - old[0, x + 1])
                new[1, x + 2] = part - 0.25 * old[1, x + 1]
                new[2, x] = part - 0.25 * old[2, x + 1]
                up = roll(part - 0.25 * old[3, x + 1], 1, 0)
                down = roll(part - 0.25 * old[4, x + 1], -1, 0)
                new[3, x + 1] = up
                new[4, x + 1] = down
                send_h[step, 2, pl.ds(x, 1), :] = up[:1]
                send_h[step, 3, pl.ds(x, 1), :] = down[cy - 1:]
                above = roll(part - 0.25 * old[5, x + 1], 1, 1)
                below = roll(part - 0.25 * old[6, x + 1], -1, 1)
                new[5, x + 1] = jnp.where(zlane == 0, 0.0, above)
                new[6, x + 1] = jnp.where(zlane == nz - 1, 0.0, below)
            return carry

        lax.fori_loop(0, cx // 2, stream, 0)
        send_h[step, 0] = new[1, cx + 1]
        send_h[step, 1] = new[2, 0]
        for n in range(4):
            @pl.when(there(*SIDES[n]))
            def _():
                halo_copy(step, n).start()

        if step == 0:
            load_blocks.wait()

            def split_block(i, carry):
                value = raw[i]
                high = value.astype(BF16)
                blocks[i, :, :BLK] = high
                blocks[i, :, BLK:] = (value - high.astype(F32)).astype(BF16)
                return carry

            lax.fori_loop(0, own * kb, split_block, 0)

        for n in range(8):
            ox, oy = OFFSETS[n]
            here = there(-ox, -oy)

            @pl.when(here)
            def _():
                ghost_copy(step, n).wait_recv()

        shell16 = lax.broadcasted_iota(jnp.int32, (SHELL, BLK), 1)
        ghost_shell = shell16 >= BLK - SHELL
        ghost_live = (shell16 >= BLK - 3 * SHELL) & (shell16 < BLK - 2 * SHELL)
        for n in range(8):
            ox, oy = OFFSETS[n]
            mark = jnp.where(ghost_live, there(-ox, -oy).astype(F32), 0.0)
            packed = recv_g[step, n]
            for j in range(BLK // SHELL):
                value = jnp.where(ghost_shell, roll(packed, BLK - (j + 1) * SHELL, 1), 0.0)
                high = high_part(value)
                marked = high + mark
                ext[own + n, j * SHELL:(j + 1) * SHELL, :] = (marked + roll(value - high, -SHELL, 1)).astype(BF16)
                ext[own + n, BLK + j * SHELL:BLK + (j + 1) * SHELL, :] = marked.astype(BF16)

        def update(c, carry):
            span = pl.ds(pl.multiple_of(c * 2 * BLK, 2 * BLK), 2 * BLK)
            temp = prof[0, span, :]
            conc = prof[1, span, :]
            mixed = []
            for d, value in enumerate((temp, conc)):
                high = value.astype(BF16)
                low = (value - high.astype(F32)).astype(BF16)
                both = dot(jnp.concatenate([high, low], axis=1), mixer[d])
                mixed.append(both[:, :BLK] + both[:, BLK:])
            totals = []
            for u in range(2):
                r = c * 2 + u
                total = dot(blocks[r * kb], ext[cols_ref[0, r]])
                for k in range(1, kb):
                    total = total + dot(blocks[r * kb + k], ext[cols_ref[k, r]])
                totals.append(total)
            total = jnp.concatenate(totals, axis=0)
            contact = total + roll(total, SHELL, 1) - roll(total, 2 * SHELL, 1) * temp
            rate = rate_c[span, :] * conc * jnp.exp(0.5 * jnp.tanh(temp - 1.0))
            new_temp = mixed[0] + rate + jnp.where(wide_lane >= BLK - SHELL, contact, 0.0)
            new_temp = new_temp + jnp.where(wide_lane == BLK - 1, cell_ex[span, :], 0.0)
            live = wide_sub + c * 2 * BLK < live_count
            prof[0, span, :] = jnp.where(live, new_temp, temp)
            prof[1, span, :] = jnp.where(live, mixed[1] - rate, conc)
            return carry

        lax.fori_loop(0, own // 2, update, 0)

        for n in range(4):
            ox, oy = SIDES[n]

            @pl.when(there(-ox, -oy))
            def _():
                halo_copy(step, n).wait_recv()

        new[1, 1] = recv_h[step, 0]
        new[2, cx] = recv_h[step, 1]

        def edges(c, carry):
            for u in range(8):
                x = c * 8 + u
                new[3, x + 1, pl.ds(0, 1), :] = recv_h[step, 2, pl.ds(x, 1), :]
                new[4, x + 1, pl.ds(cy - 1, 1), :] = recv_h[step, 3, pl.ds(x, 1), :]
            return carry

        lax.fori_loop(0, cx // 8, edges, 0)

    for step in range(STEPS):
        if step % 2 == 0:
            one_step(step, pop_a, pop_b)
        else:
            one_step(step, pop_b, pop_a)
    for step in range(STEPS):
        for n in range(8):
            @pl.when(there(*OFFSETS[n]))
            def _():
                ghost_copy(step, n).wait_send()
        for n in range(4):
            @pl.when(there(*SIDES[n]))
            def _():
                halo_copy(step, n).wait_send()


def store(prof, pop, prof_out, pop_out, sems):
    cx = pop_out.shape[1]
    store_pop = pltpu.make_async_copy(pop.at[:, pl.ds(1, cx)], pop_out, sems.at[0])
    store_prof = pltpu.make_async_copy(prof, prof_out, sems.at[1])
    store_pop.start()
    store_prof.start()
    store_pop.wait()
    store_prof.wait()


def on_device(
    profiles, radial, rate_const, transfer_coef, live_count, send_lists, cell_index, contact_cols,
    contact_blocks, populations,
):
    slots = profiles.shape[1]
    own = slots // BLK
    kb = contact_cols.shape[1]
    _, cx, cy, nz = populations.shape
    rows = cx * cy
    vmem = pl.BlockSpec(memory_space=pltpu.VMEM)
    smem = pl.BlockSpec(memory_space=pltpu.SMEM)
    anywhere = pl.BlockSpec(memory_space=pl.ANY)
    hbm = pl.BlockSpec(memory_space=pltpu.HBM)
    state = pl.pallas_call(
        kernel,
        out_shape=(
            jax.ShapeDtypeStruct(profiles.shape, F32),
            jax.ShapeDtypeStruct((7, cx + 2, cy, nz), F32),
        ),
        in_specs=[smem, smem] + [hbm] * 8,
        out_specs=(vmem, vmem),
        scratch_shapes=[
            pltpu.VMEM((7, cx + 2, cy, nz), F32),
            pltpu.VMEM((own, BLK), F32),
            pltpu.VMEM((own, BLK), F32),
            pltpu.VMEM((own, BLK), jnp.int32),
            pltpu.VMEM((8, BLK), jnp.int32),
            pltpu.VMEM((2, BLK, BLK), F32),
            pltpu.VMEM((own * kb, BLK, BLK), F32),
            pltpu.VMEM((own * kb, BLK, 2 * BLK), BF16),
            pltpu.VMEM((2, 2 * BLK, 2 * BLK), BF16),
            pltpu.VMEM((slots, rows), BF16),
            pltpu.VMEM((rows, slots), BF16),
            pltpu.VMEM((8 * BLK, slots), BF16),
            pltpu.VMEM((slots, nz), F32),
            pltpu.VMEM((slots, BLK), F32),
            pltpu.VMEM((slots, BLK), F32),
            pltpu.VMEM((slots, BLK), BF16),
            pltpu.VMEM((own + 8, 2 * BLK, BLK), BF16),
            pltpu.VMEM((cx, cy, nz), F32),
            pltpu.VMEM((rows, 2 * nz), BF16),
            pltpu.VMEM((slots, BLK), F32),
            pltpu.VMEM((slots, 2 * nz), BF16),
            pltpu.VMEM((cx, cy, nz), F32),
            pltpu.VMEM((STEPS, 8, SHELL, BLK), F32),
            pltpu.VMEM((STEPS, 8, SHELL, BLK), F32),
            pltpu.VMEM((STEPS, 4, cx, nz), F32),
            pltpu.VMEM((STEPS, 4, cx, nz), F32),
            pltpu.SemaphoreType.DMA((8,)),
            pltpu.SemaphoreType.DMA((STEPS, 8)),
            pltpu.SemaphoreType.DMA((STEPS, 8)),
            pltpu.SemaphoreType.DMA((STEPS, 4)),
            pltpu.SemaphoreType.DMA((STEPS, 4)),
        ],
        compiler_params=pltpu.CompilerParams(
            collective_id=0, has_side_effects=True, vmem_limit_bytes=36 * 1024 * 1024
        ),
    )(
        live_count,
        pltpu.with_memory_space_constraint(contact_cols.T, pltpu.HBM),
        *[
            pltpu.with_memory_space_constraint(operand, pltpu.HBM)
            for operand in (
                rate_const.reshape(own, BLK),
                transfer_coef.reshape(own, BLK),
                cell_index.reshape(own, BLK),
                send_lists,
                radial,
                profiles,
                contact_blocks.reshape(own * kb, BLK, BLK),
                populations,
            )
        ],
    )
    return pl.pallas_call(
        store,
        out_shape=(
            jax.ShapeDtypeStruct(profiles.shape, F32),
            jax.ShapeDtypeStruct(populations.shape, F32),
        ),
        in_specs=[anywhere, anywhere],
        out_specs=(hbm, hbm),
        scratch_shapes=[pltpu.SemaphoreType.DMA((2,))],
        compiler_params=pltpu.CompilerParams(vmem_limit_bytes=1024 * 1024),
    )(*state)


def solution(mesh):
    return jax.shard_map(
        on_device,
        mesh=mesh,
        in_specs=(
            P(None, ("gx", "gy"), None),
            P(),
            P(("gx", "gy")),
            P(("gx", "gy")),
            P(("gx", "gy")),
            P(("gx", "gy"), None),
            P(("gx", "gy")),
            P(("gx", "gy"), None),
            P(("gx", "gy"), None, None, None),
            P(None, "gx", "gy", None),
        ),
        out_specs=(P(None, ("gx", "gy"), None), P(None, "gx", "gy", None)),
        check_vma=False,
    )
```

```python
import jax
import jax.numpy as jnp
import numpy as np
from jax import lax
from jax.experimental import pallas as pl
from jax.experimental.pallas import tpu as pltpu
from jax.sharding import PartitionSpec as P

BLK = 128
SHELL = 16
STEPS = 3
OFFSETS = ((-1, -1), (-1, 0), (-1, 1), (0, -1), (0, 1), (1, -1), (1, 0), (1, 1))
SIDES = ((1, 0), (-1, 0), (0, 1), (0, -1))
MESH = pl.DeviceIdType.MESH
F32 = jnp.float32
BF16 = jnp.bfloat16


def high_part(value):
    return value.astype(BF16).astype(F32)


def dot(a, b):
    return jnp.dot(a, b, preferred_element_type=F32)


def roll(value, amount, axis):
    amount = amount % value.shape[axis]
    return value if amount == 0 else pltpu.roll(value, amount, axis)


def kernel(
    live_ref, cols_ref, rate_in, coef_in, cell_in, lists_in, radial_in,
    prof_in, blocks_in, pop_in,
    prof, pop_b,
    pop_a, rate_ref, coef_ref, cell_ref, lists_ref, radial_ref,
    raw, blocks, mixer, pick, pick_t, listed, zmask, coef, rate_c,
    shells, ext, theta, theta_s, cell_ex, ex_s,
    send_g, recv_g, send_h, recv_h,
    in_sems, gs_sems, gr_sems, hs_sems, hr_sems,
):
    own = prof.shape[1] // BLK
    cx, cy, nz = theta.shape
    rows = cx * cy
    kb = cols_ref.shape[0]
    ix, iy = lax.axis_index("gx"), lax.axis_index("gy")
    sx, sy = lax.axis_size("gx"), lax.axis_size("gy")

    def there(ox, oy):
        x, y = ix + ox, iy + oy
        return (x >= 0) & (x < sx) & (y >= 0) & (y < sy)

    small = [
        pltpu.make_async_copy(source, target, in_sems.at[3 + i])
        for i, (source, target) in enumerate((
            (lists_in, lists_ref), (cell_in, cell_ref), (coef_in, coef_ref), (rate_in, rate_ref),
            (radial_in, radial_ref)))
    ]
    load_prof = pltpu.make_async_copy(prof_in, prof, in_sems.at[0])
    load_pop = pltpu.make_async_copy(pop_in, pop_a.at[:, pl.ds(1, cx)], in_sems.at[1])
    load_blocks = pltpu.make_async_copy(blocks_in, raw, in_sems.at[2])
    for load in small:
        load.start()
    load_prof.start()
    load_pop.start()
    load_blocks.start()

    recv_g[...] = jnp.zeros_like(recv_g)
    recv_h[...] = jnp.zeros_like(recv_h)
    barrier = pltpu.get_barrier_semaphore()
    for ox, oy in OFFSETS:
        @pl.when(there(ox, oy))
        def _():
            pl.semaphore_signal(barrier, inc=1, device_id=(ix + ox, iy + oy), device_id_type=MESH)

    live_count = live_ref[0]
    sub = lax.broadcasted_iota(jnp.int32, (BLK, BLK), 0)
    lane = lax.broadcasted_iota(jnp.int32, (BLK, BLK), 1)
    lane_f = lane.astype(F32)
    sub_f = sub.astype(F32)
    wide_sub = lax.broadcasted_iota(jnp.int32, (2 * BLK, BLK), 0)
    wide_lane = lax.broadcasted_iota(jnp.int32, (2 * BLK, BLK), 1)
    in_shell = lane >= BLK - SHELL
    in_live = (lane >= BLK - 3 * SHELL) & (lane < BLK - 2 * SHELL)

    def one_hot(match):
        return jnp.where(match, 1.0, 0.0).astype(BF16)

    def column(row):
        return jnp.broadcast_to(row, (BLK, BLK)).T

    for load in small:
        load.wait()

    def setup(c, carry):
        span = pl.ds(pl.multiple_of(c * BLK, BLK), BLK)
        at = pl.ds(c, 1)
        cell = cell_ref[at, :]
        row_col = column((cell // nz).astype(F32))
        z_col = column((cell % nz).astype(F32))
        list_col = column(lists_ref[at, :].astype(F32))
        zmask[span, :] = jnp.where(z_col == lane_f, 1.0, 0.0)
        coef[span, :] = jnp.where(sub + c * BLK < live_count, column(coef_ref[at, :]), 0.0)
        rate_c[span, :] = column(rate_ref[at, :])
        for d in range(rows // BLK):
            pick[span, d * BLK:(d + 1) * BLK] = one_hot(row_col == lane_f + d * BLK)
        for d in range(own):
            listed[span, d * BLK:(d + 1) * BLK] = one_hot(list_col == lane_f + d * BLK)
        return carry

    lax.fori_loop(0, own, setup, 0)

    def setup_t(c, carry):
        span = pl.ds(pl.multiple_of(c * BLK, BLK), BLK)
        base = sub_f + (c * BLK).astype(F32)
        for d in range(own):
            row = (cell_ref[d:d + 1, :] // nz).astype(F32)
            pick_t[span, d * BLK:(d + 1) * BLK] = one_hot(jnp.broadcast_to(row, (BLK, BLK)) == base)
        return carry

    lax.fori_loop(0, rows // BLK, setup_t, 0)

    for c in range(2):
        value = radial_ref[c]
        high = value.astype(BF16)
        low = (value - high.astype(F32)).astype(BF16)
        mixer[c, :BLK, :BLK] = high
        mixer[c, :BLK, BLK:] = low
        mixer[c, BLK:, :BLK] = high
        mixer[c, BLK:, BLK:] = jnp.zeros_like(high)

    load_prof.wait()
    count_x = 1 + (ix > 0).astype(jnp.int32) + (ix < sx - 1).astype(jnp.int32)
    count_y = 1 + (iy > 0).astype(jnp.int32) + (iy < sy - 1).astype(jnp.int32)
    pl.semaphore_wait(barrier, count_x * count_y - 1)

    def ghost_copy(step, n):
        ox, oy = OFFSETS[n]
        return pltpu.make_async_remote_copy(
            src_ref=send_g.at[step, n], dst_ref=recv_g.at[step, n],
            send_sem=gs_sems.at[step, n], recv_sem=gr_sems.at[step, n],
            device_id=(ix + ox, iy + oy), device_id_type=MESH)

    def halo_copy(step, n):
        ox, oy = SIDES[n]
        return pltpu.make_async_remote_copy(
            src_ref=send_h.at[step, n], dst_ref=recv_h.at[step, n],
            send_sem=hs_sems.at[step, n], recv_sem=hr_sems.at[step, n],
            device_id=(ix + ox, iy + oy), device_id_type=MESH)

    def one_step(step, old, new):
        def prepare(r, carry):
            span = pl.ds(pl.multiple_of(r * BLK, BLK), BLK)
            value = jnp.where(in_shell, prof[0, span, :], 0.0)
            high = high_part(value)
            low = value - high
            mid = high_part(low)
            low_rolled = roll(low, -SHELL, 1)
            shells[span, :] = (high + roll(mid, -SHELL, 1) + roll(low - mid, -2 * SHELL, 1)).astype(BF16)
            live = sub + r * BLK < live_count
            marked = high + jnp.where(in_live, 1.0, 0.0)
            ext[r, :BLK, :] = jnp.where(live, marked + low_rolled, 0.0).astype(BF16)
            ext[r, BLK:, :] = jnp.where(live, marked, 0.0).astype(BF16)
            return carry

        lax.fori_loop(0, own, prepare, 0)

        if step == 0:
            load_pop.wait()

        def ghosts_and_theta(n, carry):
            span = pl.ds(pl.multiple_of(n * 4 * BLK, 4 * BLK), 4 * BLK)
            several = dot(listed[span, :], shells[...])
            for u in range(cx // 2):
                x = n * (cx // 2) + u
                total = old[0, x + 1]
                for i in range(1, 7):
                    total = total + old[i, x + 1]
                theta[x] = total
                at = pl.ds(pl.multiple_of(x * cy, cy), cy)
                high = total.astype(BF16)
                theta_s[at, :nz] = high
                theta_s[at, nz:] = (total - high.astype(F32)).astype(BF16)
            for m in range(4):
                found = several[m * BLK:(m + 1) * BLK, :]
                found = found + roll(found, SHELL, 1) + roll(found, 2 * SHELL, 1)
                found = jnp.where(in_shell, found, 0.0)
                packed = jnp.zeros((SHELL, BLK), F32)
                for j in range(BLK // SHELL):
                    packed = packed + roll(found[j * SHELL:(j + 1) * SHELL, :], (j + 1) * SHELL, 1)
                send_g[step, n * 4 + m] = packed
            return carry

        lax.fori_loop(0, 2, ghosts_and_theta, 0)
        for n in range(8):
            @pl.when(there(*OFFSETS[n]))
            def _():
                ghost_copy(step, n).start()

        ones = jnp.ones((2 * nz, BLK), BF16)

        def gather_theta(c, carry):
            span = pl.ds(pl.multiple_of(c * 4 * BLK, 4 * BLK), 4 * BLK)
            found = dot(pick[span, :], theta_s[...])
            mask = zmask[span, :]
            kept = jnp.concatenate([found[:, :nz] * mask, found[:, nz:] * mask], axis=1).astype(BF16)
            at_cell = dot(kept, ones)
            last = jnp.broadcast_to(prof[0, span, BLK - 1:], (4 * BLK, BLK))
            value = coef[span, :] * (at_cell - last)
            cell_ex[span, :] = value
            value = value * mask
            high = value.astype(BF16)
            ex_s[span, :nz] = high
            ex_s[span, nz:] = (value - high.astype(F32)).astype(BF16)
            return carry

        lax.fori_loop(0, own // 4, gather_theta, 0)
        slabs = 2 * BLK // cy
        zlane = lax.broadcasted_iota(jnp.int32, (cy, nz), 1)

        def scatter_and_stream(c, carry):
            founds = []
            for v in range(2):
                start = pl.multiple_of((c * 2 + v) * 2 * BLK, 2 * BLK)
                founds.append(dot(pick_t[pl.ds(start, 2 * BLK), :], ex_s[...]))
            for v in range(2):
                source = founds[v][:, :nz] + founds[v][:, nz:]
                for u in range(slabs):
                    x = (c * 2 + v) * slabs + u
                    q = 1.25 * theta[x] - 0.5 * source[u * cy:(u + 1) * cy, :]
                    part = 0.125 * q
                    new[0, x + 1] = 0.25 * (q - old[0, x + 1])
                    new[1, x + 2] = part - 0.25 * old[1, x + 1]
                    new[2, x] = part - 0.25 * old[2, x + 1]
                    up = roll(part - 0.25 * old[3, x + 1], 1, 0)
                    down = roll(part - 0.25 * old[4, x + 1], -1, 0)
                    new[3, x + 1] = up
                    new[4, x + 1] = down
                    send_h[step, 2, pl.ds(x, 1), :] = up[:1]
                    send_h[step, 3, pl.ds(x, 1), :] = down[cy - 1:]
                    above = roll(part - 0.25 * old[5, x + 1], 1, 1)
                    below = roll(part - 0.25 * old[6, x + 1], -1, 1)
                    new[5, x + 1] = jnp.where(zlane == 0, 0.0, above)
                    new[6, x + 1] = jnp.where(zlane == nz - 1, 0.0, below)
            return carry

        lax.fori_loop(0, rows // (4 * BLK), scatter_and_stream, 0)
        send_h[step, 0] = new[1, cx + 1]
        send_h[step, 1] = new[2, 0]
        for n in range(4):
            @pl.when(there(*SIDES[n]))
            def _():
                halo_copy(step, n).start()

        if step == 0:
            load_blocks.wait()

            def split_blocks(r, carry):
                for k in range(kb):
                    value = raw[r * kb + k]
                    high = value.astype(BF16)
                    blocks[r * kb + k, :, :BLK] = high
                    blocks[r * kb + k, :, BLK:] = (value - high.astype(F32)).astype(BF16)
                return carry

            lax.fori_loop(0, own, split_blocks, 0)

        for n in range(8):
            ox, oy = OFFSETS[n]
            here = there(-ox, -oy)

            @pl.when(here)
            def _():
                ghost_copy(step, n).wait_recv()

        shell16 = lax.broadcasted_iota(jnp.int32, (SHELL, BLK), 1)
        ghost_shell = shell16 >= BLK - SHELL
        ghost_live = (shell16 >= BLK - 3 * SHELL) & (shell16 < BLK - 2 * SHELL)
        for n in range(8):
            ox, oy = OFFSETS[n]
            mark = jnp.where(ghost_live, there(-ox, -oy).astype(F32), 0.0)
            packed = recv_g[step, n]
            for j in range(BLK // SHELL):
                value = jnp.where(ghost_shell, roll(packed, BLK - (j + 1) * SHELL, 1), 0.0)
                high = high_part(value)
                marked = high + mark
                ext[own + n, j * SHELL:(j + 1) * SHELL, :] = (marked + roll(value - high, -SHELL, 1)).astype(BF16)
                ext[own + n, BLK + j * SHELL:BLK + (j + 1) * SHELL, :] = marked.astype(BF16)

        def update(c):
            span = pl.ds(c * 2 * BLK, 2 * BLK)
            temp = prof[0, span, :]
            conc = prof[1, span, :]
            mixed = []
            for d, value in enumerate((temp, conc)):
                high = value.astype(BF16)
                low = (value - high.astype(F32)).astype(BF16)
                both = dot(jnp.concatenate([high, low], axis=1), mixer[d])
                mixed.append(both[:, :BLK] + both[:, BLK:])
            totals = []
            for u in range(2):
                r = c * 2 + u
                total = dot(blocks[r * kb], ext[cols_ref[0, r]])
                for k in range(1, kb):
                    total = total + dot(blocks[r * kb + k], ext[cols_ref[k, r]])
                totals.append(total)
            total = jnp.concatenate(totals, axis=0)
            contact = total + roll(total, SHELL, 1) - roll(total, 2 * SHELL, 1) * temp
            rate = rate_c[span, :] * conc * jnp.exp(0.5 * jnp.tanh(temp - 1.0))
            new_temp = mixed[0] + rate + jnp.where(wide_lane >= BLK - SHELL, contact, 0.0)
            new_temp = new_temp + jnp.where(wide_lane == BLK - 1, cell_ex[span, :], 0.0)
            live = wide_sub + c * 2 * BLK < live_count
            prof[0, span, :] = jnp.where(live, new_temp, temp)
            prof[1, span, :] = jnp.where(live, mixed[1] - rate, conc)

        for c in range(own // 2):
            update(c)

        for n in range(4):
            ox, oy = SIDES[n]

            @pl.when(there(-ox, -oy))
            def _():
                halo_copy(step, n).wait_recv()

        new[1, 1] = recv_h[step, 0]
        new[2, cx] = recv_h[step, 1]

        def edges(c, carry):
            for u in range(8):
                x = c * 8 + u
                new[3, x + 1, pl.ds(0, 1), :] = recv_h[step, 2, pl.ds(x, 1), :]
                new[4, x + 1, pl.ds(cy - 1, 1), :] = recv_h[step, 3, pl.ds(x, 1), :]
            return carry

        lax.fori_loop(0, cx // 8, edges, 0)

    for step in range(STEPS):
        if step % 2 == 0:
            one_step(step, pop_a, pop_b)
        else:
            one_step(step, pop_b, pop_a)
    for step in range(STEPS):
        for n in range(8):
            @pl.when(there(*OFFSETS[n]))
            def _():
                ghost_copy(step, n).wait_send()
        for n in range(4):
            @pl.when(there(*SIDES[n]))
            def _():
                halo_copy(step, n).wait_send()


def store(prof, pop, prof_out, pop_out, sems):
    cx = pop_out.shape[1]
    store_pop = pltpu.make_async_copy(pop.at[:, pl.ds(1, cx)], pop_out, sems.at[0])
    store_prof = pltpu.make_async_copy(prof, prof_out, sems.at[1])
    store_pop.start()
    store_prof.start()
    store_pop.wait()
    store_prof.wait()


def on_device(
    profiles, radial, rate_const, transfer_coef, live_count, send_lists, cell_index, contact_cols,
    contact_blocks, populations,
):
    slots = profiles.shape[1]
    own = slots // BLK
    kb = contact_cols.shape[1]
    _, cx, cy, nz = populations.shape
    rows = cx * cy
    vmem = pl.BlockSpec(memory_space=pltpu.VMEM)
    smem = pl.BlockSpec(memory_space=pltpu.SMEM)
    anywhere = pl.BlockSpec(memory_space=pl.ANY)
    hbm = pl.BlockSpec(memory_space=pltpu.HBM)
    state = pl.pallas_call(
        kernel,
        out_shape=(
            jax.ShapeDtypeStruct(profiles.shape, F32),
            jax.ShapeDtypeStruct((7, cx + 2, cy, nz), F32),
        ),
        in_specs=[smem, smem] + [hbm] * 8,
        out_specs=(vmem, vmem),
        scratch_shapes=[
            pltpu.VMEM((7, cx + 2, cy, nz), F32),
            pltpu.VMEM((own, BLK), F32),
            pltpu.VMEM((own, BLK), F32),
            pltpu.VMEM((own, BLK), jnp.int32),
            pltpu.VMEM((8, BLK), jnp.int32),
            pltpu.VMEM((2, BLK, BLK), F32),
            pltpu.VMEM((own * kb, BLK, BLK), F32),
            pltpu.VMEM((own * kb, BLK, 2 * BLK), BF16),
            pltpu.VMEM((2, 2 * BLK, 2 * BLK), BF16),
            pltpu.VMEM((slots, rows), BF16),
            pltpu.VMEM((rows, slots), BF16),
            pltpu.VMEM((8 * BLK, slots), BF16),
            pltpu.VMEM((slots, nz), F32),
            pltpu.VMEM((slots, BLK), F32),
            pltpu.VMEM((slots, BLK), F32),
            pltpu.VMEM((slots, BLK), BF16),
            pltpu.VMEM((own + 8, 2 * BLK, BLK), BF16),
            pltpu.VMEM((cx, cy, nz), F32),
            pltpu.VMEM((rows, 2 * nz), BF16),
            pltpu.VMEM((slots, BLK), F32),
            pltpu.VMEM((slots, 2 * nz), BF16),
            pltpu.VMEM((STEPS, 8, SHELL, BLK), F32),
            pltpu.VMEM((STEPS, 8, SHELL, BLK), F32),
            pltpu.VMEM((STEPS, 4, cx, nz), F32),
            pltpu.VMEM((STEPS, 4, cx, nz), F32),
            pltpu.SemaphoreType.DMA((8,)),
            pltpu.SemaphoreType.DMA((STEPS, 8)),
            pltpu.SemaphoreType.DMA((STEPS, 8)),
            pltpu.SemaphoreType.DMA((STEPS, 4)),
            pltpu.SemaphoreType.DMA((STEPS, 4)),
        ],
        compiler_params=pltpu.CompilerParams(
            collective_id=0, has_side_effects=True, vmem_limit_bytes=36 * 1024 * 1024
        ),
    )(
        live_count,
        pltpu.with_memory_space_constraint(contact_cols.T, pltpu.HBM),
        *[
            pltpu.with_memory_space_constraint(operand, pltpu.HBM)
            for operand in (
                rate_const.reshape(own, BLK),
                transfer_coef.reshape(own, BLK),
                cell_index.reshape(own, BLK),
                send_lists,
                radial,
                profiles,
                contact_blocks.reshape(own * kb, BLK, BLK),
                populations,
            )
        ],
    )
    return pl.pallas_call(
        store,
        out_shape=(
            jax.ShapeDtypeStruct(profiles.shape, F32),
            jax.ShapeDtypeStruct(populations.shape, F32),
        ),
        in_specs=[anywhere, anywhere],
        out_specs=(hbm, hbm),
        scratch_shapes=[pltpu.SemaphoreType.DMA((2,))],
        compiler_params=pltpu.CompilerParams(vmem_limit_bytes=1024 * 1024),
    )(*state)


def solution(mesh):
    return jax.shard_map(
        on_device,
        mesh=mesh,
        in_specs=(
            P(None, ("gx", "gy"), None),
            P(),
            P(("gx", "gy")),
            P(("gx", "gy")),
            P(("gx", "gy")),
            P(("gx", "gy"), None),
            P(("gx", "gy")),
            P(("gx", "gy"), None),
            P(("gx", "gy"), None, None, None),
            P(None, "gx", "gy", None),
        ),
        out_specs=(P(None, ("gx", "gy"), None), P(None, "gx", "gy", None)),
        check_vma=False,
    )
```

```python
import jax
import jax.numpy as jnp
import numpy as np
from jax import lax
from jax.experimental import pallas as pl
from jax.experimental.pallas import tpu as pltpu
from jax.sharding import PartitionSpec as P

BLK = 128
SHELL = 16
STEPS = 3
OFFSETS = ((-1, -1), (-1, 0), (-1, 1), (0, -1), (0, 1), (1, -1), (1, 0), (1, 1))
SIDES = ((1, 0), (-1, 0), (0, 1), (0, -1))
MESH = pl.DeviceIdType.MESH
F32 = jnp.float32
BF16 = jnp.bfloat16


def high_part(value):
    return value.astype(BF16).astype(F32)


def dot(a, b):
    return jnp.dot(a, b, preferred_element_type=F32)


def roll(value, amount, axis):
    amount = amount % value.shape[axis]
    return value if amount == 0 else pltpu.roll(value, amount, axis)


def kernel(
    live_ref, cols_ref, rate_in, coef_in, cell_in, lists_in, radial_in,
    prof_in, blocks_in, pop_in,
    prof, pop_b,
    pop_a, rate_ref, coef_ref, cell_ref, lists_ref, radial_ref,
    raw, blocks, mixer, pick, pick_t, listed, zmask, coef, rate_c,
    shells, ext, theta, theta_s, cell_ex, ex_s, fresh,
    send_g, recv_g, send_h, recv_h,
    in_sems, gs_sems, gr_sems, hs_sems, hr_sems,
):
    own = prof.shape[1] // BLK
    cx, cy, nz = theta.shape
    rows = cx * cy
    kb = cols_ref.shape[0]
    ix, iy = lax.axis_index("gx"), lax.axis_index("gy")
    sx, sy = lax.axis_size("gx"), lax.axis_size("gy")

    def there(ox, oy):
        x, y = ix + ox, iy + oy
        return (x >= 0) & (x < sx) & (y >= 0) & (y < sy)

    small = [
        pltpu.make_async_copy(source, target, in_sems.at[3 + i])
        for i, (source, target) in enumerate((
            (lists_in, lists_ref), (cell_in, cell_ref), (coef_in, coef_ref), (rate_in, rate_ref),
            (radial_in, radial_ref)))
    ]
    load_prof = pltpu.make_async_copy(prof_in, prof, in_sems.at[0])
    load_pop = pltpu.make_async_copy(pop_in, pop_a.at[:, pl.ds(1, cx)], in_sems.at[1])
    load_blocks = pltpu.make_async_copy(blocks_in, raw, in_sems.at[2])
    for load in small:
        load.start()
    load_prof.start()
    load_pop.start()
    load_blocks.start()

    recv_g[...] = jnp.zeros_like(recv_g)
    recv_h[...] = jnp.zeros_like(recv_h)
    barrier = pltpu.get_barrier_semaphore()
    for ox, oy in OFFSETS:
        @pl.when(there(ox, oy))
        def _():
            pl.semaphore_signal(barrier, inc=1, device_id=(ix + ox, iy + oy), device_id_type=MESH)

    live_count = live_ref[0]
    sub = lax.broadcasted_iota(jnp.int32, (BLK, BLK), 0)
    lane = lax.broadcasted_iota(jnp.int32, (BLK, BLK), 1)
    lane_f = lane.astype(F32)
    sub_f = sub.astype(F32)
    wide_sub = lax.broadcasted_iota(jnp.int32, (2 * BLK, BLK), 0)
    wide_lane = lax.broadcasted_iota(jnp.int32, (2 * BLK, BLK), 1)
    in_shell = lane >= BLK - SHELL
    in_live = (lane >= BLK - 3 * SHELL) & (lane < BLK - 2 * SHELL)

    def one_hot(match):
        return jnp.where(match, 1.0, 0.0).astype(BF16)

    def column(row):
        return jnp.broadcast_to(row, (BLK, BLK)).T

    for load in small:
        load.wait()

    def setup(c, carry):
        span = pl.ds(pl.multiple_of(c * BLK, BLK), BLK)
        at = pl.ds(c, 1)
        cell = cell_ref[at, :]
        row_col = column((cell // nz).astype(F32))
        z_col = column((cell % nz).astype(F32))
        list_col = column(lists_ref[at, :].astype(F32))
        zmask[span, :] = jnp.where(z_col == lane_f, 1.0, 0.0)
        coef[span, :] = jnp.where(sub + c * BLK < live_count, column(coef_ref[at, :]), 0.0)
        rate_c[span, :] = column(rate_ref[at, :])
        for d in range(rows // BLK):
            pick[span, d * BLK:(d + 1) * BLK] = one_hot(row_col == lane_f + d * BLK)
        for d in range(own):
            listed[span, d * BLK:(d + 1) * BLK] = one_hot(list_col == lane_f + d * BLK)
        return carry

    lax.fori_loop(0, own, setup, 0)

    def setup_t(c, carry):
        span = pl.ds(pl.multiple_of(c * BLK, BLK), BLK)
        base = sub_f + (c * BLK).astype(F32)
        for d in range(own):
            row = (cell_ref[d:d + 1, :] // nz).astype(F32)
            pick_t[span, d * BLK:(d + 1) * BLK] = one_hot(jnp.broadcast_to(row, (BLK, BLK)) == base)
        return carry

    lax.fori_loop(0, rows // BLK, setup_t, 0)

    for c in range(2):
        value = radial_ref[c]
        high = value.astype(BF16)
        low = (value - high.astype(F32)).astype(BF16)
        mixer[c, :BLK, :BLK] = high
        mixer[c, :BLK, BLK:] = low
        mixer[c, BLK:, :BLK] = high
        mixer[c, BLK:, BLK:] = jnp.zeros_like(high)

    load_prof.wait()
    count_x = 1 + (ix > 0).astype(jnp.int32) + (ix < sx - 1).astype(jnp.int32)
    count_y = 1 + (iy > 0).astype(jnp.int32) + (iy < sy - 1).astype(jnp.int32)
    pl.semaphore_wait(barrier, count_x * count_y - 1)

    def ghost_copy(step, n):
        ox, oy = OFFSETS[n]
        return pltpu.make_async_remote_copy(
            src_ref=send_g.at[step, n], dst_ref=recv_g.at[step, n],
            send_sem=gs_sems.at[step, n], recv_sem=gr_sems.at[step, n],
            device_id=(ix + ox, iy + oy), device_id_type=MESH)

    def halo_copy(step, n):
        ox, oy = SIDES[n]
        return pltpu.make_async_remote_copy(
            src_ref=send_h.at[step, n], dst_ref=recv_h.at[step, n],
            send_sem=hs_sems.at[step, n], recv_sem=hr_sems.at[step, n],
            device_id=(ix + ox, iy + oy), device_id_type=MESH)

    def one_step(step, old, new):
        def prepare(r, carry):
            span = pl.ds(pl.multiple_of(r * BLK, BLK), BLK)
            value = jnp.where(in_shell, prof[0, span, :], 0.0)
            high = high_part(value)
            low = value - high
            mid = high_part(low)
            low_rolled = roll(low, -SHELL, 1)
            shells[span, :] = (high + roll(mid, -SHELL, 1) + roll(low - mid, -2 * SHELL, 1)).astype(BF16)
            live = sub + r * BLK < live_count
            marked = high + jnp.where(in_live, 1.0, 0.0)
            ext[r, :BLK, :] = jnp.where(live, marked + low_rolled, 0.0).astype(BF16)
            ext[r, BLK:, :] = jnp.where(live, marked, 0.0).astype(BF16)
            return carry

        lax.fori_loop(0, own, prepare, 0)

        if step == 0:
            load_pop.wait()

        def ghosts_and_theta(n, carry):
            span = pl.ds(pl.multiple_of(n * 4 * BLK, 4 * BLK), 4 * BLK)
            several = dot(listed[span, :], shells[...])
            for u in range(cx // 2):
                x = n * (cx // 2) + u
                total = old[0, x + 1]
                for i in range(1, 7):
                    total = total + old[i, x + 1]
                theta[x] = total
                at = pl.ds(pl.multiple_of(x * cy, cy), cy)
                high = total.astype(BF16)
                theta_s[at, :nz] = high
                theta_s[at, nz:] = (total - high.astype(F32)).astype(BF16)
            for m in range(4):
                found = several[m * BLK:(m + 1) * BLK, :]
                found = found + roll(found, SHELL, 1) + roll(found, 2 * SHELL, 1)
                found = jnp.where(in_shell, found, 0.0)
                packed = jnp.zeros((SHELL, BLK), F32)
                for j in range(BLK // SHELL):
                    packed = packed + roll(found[j * SHELL:(j + 1) * SHELL, :], (j + 1) * SHELL, 1)
                send_g[step, n * 4 + m] = packed
            return carry

        lax.fori_loop(0, 2, ghosts_and_theta, 0)
        for n in range(8):
            @pl.when(there(*OFFSETS[n]))
            def _():
                ghost_copy(step, n).start()

        ones = jnp.ones((2 * nz, BLK), BF16)

        def gather_theta(c, carry):
            span = pl.ds(pl.multiple_of(c * 4 * BLK, 4 * BLK), 4 * BLK)
            found = dot(pick[span, :], theta_s[...])
            mask = zmask[span, :]
            kept = jnp.concatenate([found[:, :nz] * mask, found[:, nz:] * mask], axis=1).astype(BF16)
            at_cell = dot(kept, ones)
            temp = prof[0, span, :]
            conc = prof[1, span, :]
            mixed = []
            for d, part in enumerate((temp, conc)):
                high = part.astype(BF16)
                low = (part - high.astype(F32)).astype(BF16)
                both = dot(jnp.concatenate([high, low], axis=1), mixer[d])
                mixed.append(both[:, :BLK] + both[:, BLK:])
            rate = rate_c[span, :] * conc * jnp.exp(0.5 * jnp.tanh(temp - 1.0))
            fresh[span, :] = mixed[0] + rate
            live = lax.broadcasted_iota(jnp.int32, (4 * BLK, BLK), 0) + c * 4 * BLK < live_count
            prof[1, span, :] = jnp.where(live, mixed[1] - rate, conc)
            last = jnp.broadcast_to(temp[:, BLK - 1:], (4 * BLK, BLK))
            value = coef[span, :] * (at_cell - last)
            cell_ex[span, :] = value
            value = value * mask
            high = value.astype(BF16)
            ex_s[span, :nz] = high
            ex_s[span, nz:] = (value - high.astype(F32)).astype(BF16)
            return carry

        lax.fori_loop(0, own // 4, gather_theta, 0)
        slabs = 2 * BLK // cy
        zlane = lax.broadcasted_iota(jnp.int32, (cy, nz), 1)

        def scatter_and_stream(c, carry):
            founds = []
            for v in range(2):
                start = pl.multiple_of((c * 2 + v) * 2 * BLK, 2 * BLK)
                founds.append(dot(pick_t[pl.ds(start, 2 * BLK), :], ex_s[...]))
            for v in range(2):
                source = founds[v][:, :nz] + founds[v][:, nz:]
                for u in range(slabs):
                    x = (c * 2 + v) * slabs + u
                    q = 1.25 * theta[x] - 0.5 * source[u * cy:(u + 1) * cy, :]
                    part = 0.125 * q
                    new[0, x + 1] = 0.25 * (q - old[0, x + 1])
                    new[1, x + 2] = part - 0.25 * old[1, x + 1]
                    new[2, x] = part - 0.25 * old[2, x + 1]
                    up = roll(part - 0.25 * old[3, x + 1], 1, 0)
                    down = roll(part - 0.25 * old[4, x + 1], -1, 0)
                    new[3, x + 1] = up
                    new[4, x + 1] = down
                    send_h[step, 2, pl.ds(x, 1), :] = up[:1]
                    send_h[step, 3, pl.ds(x, 1), :] = down[cy - 1:]
                    above = roll(part - 0.25 * old[5, x + 1], 1, 1)
                    below = roll(part - 0.25 * old[6, x + 1], -1, 1)
                    new[5, x + 1] = jnp.where(zlane == 0, 0.0, above)
                    new[6, x + 1] = jnp.where(zlane == nz - 1, 0.0, below)
            return carry

        lax.fori_loop(0, rows // (4 * BLK), scatter_and_stream, 0)
        send_h[step, 0] = new[1, cx + 1]
        send_h[step, 1] = new[2, 0]
        for n in range(4):
            @pl.when(there(*SIDES[n]))
            def _():
                halo_copy(step, n).start()

        if step == 0:
            load_blocks.wait()

            def split_blocks(r, carry):
                for k in range(kb):
                    value = raw[r * kb + k]
                    high = value.astype(BF16)
                    blocks[r * kb + k, :, :BLK] = high
                    blocks[r * kb + k, :, BLK:] = (value - high.astype(F32)).astype(BF16)
                return carry

            lax.fori_loop(0, own, split_blocks, 0)

        for n in range(8):
            ox, oy = OFFSETS[n]
            here = there(-ox, -oy)

            @pl.when(here)
            def _():
                ghost_copy(step, n).wait_recv()

        shell16 = lax.broadcasted_iota(jnp.int32, (SHELL, BLK), 1)
        ghost_shell = shell16 >= BLK - SHELL
        ghost_live = (shell16 >= BLK - 3 * SHELL) & (shell16 < BLK - 2 * SHELL)
        for n in range(8):
            ox, oy = OFFSETS[n]
            mark = jnp.where(ghost_live, there(-ox, -oy).astype(F32), 0.0)
            packed = recv_g[step, n]
            for j in range(BLK // SHELL):
                value = jnp.where(ghost_shell, roll(packed, BLK - (j + 1) * SHELL, 1), 0.0)
                high = high_part(value)
                marked = high + mark
                ext[own + n, j * SHELL:(j + 1) * SHELL, :] = (marked + roll(value - high, -SHELL, 1)).astype(BF16)
                ext[own + n, BLK + j * SHELL:BLK + (j + 1) * SHELL, :] = marked.astype(BF16)

        def update(c):
            span = pl.ds(c * 2 * BLK, 2 * BLK)
            temp = prof[0, span, :]
            totals = []
            for u in range(2):
                r = c * 2 + u
                total = dot(blocks[r * kb], ext[cols_ref[0, r]])
                for k in range(1, kb):
                    total = total + dot(blocks[r * kb + k], ext[cols_ref[k, r]])
                totals.append(total)
            total = jnp.concatenate(totals, axis=0)
            contact = total + roll(total, SHELL, 1) - roll(total, 2 * SHELL, 1) * temp
            new_temp = fresh[span, :] + jnp.where(wide_lane >= BLK - SHELL, contact, 0.0)
            new_temp = new_temp + jnp.where(wide_lane == BLK - 1, cell_ex[span, :], 0.0)
            live = wide_sub + c * 2 * BLK < live_count
            prof[0, span, :] = jnp.where(live, new_temp, temp)

        for c in range(own // 2):
            update(c)

        for n in range(4):
            ox, oy = SIDES[n]

            @pl.when(there(-ox, -oy))
            def _():
                halo_copy(step, n).wait_recv()

        new[1, 1] = recv_h[step, 0]
        new[2, cx] = recv_h[step, 1]

        def edges(c, carry):
            for u in range(8):
                x = c * 8 + u
                new[3, x + 1, pl.ds(0, 1), :] = recv_h[step, 2, pl.ds(x, 1), :]
                new[4, x + 1, pl.ds(cy - 1, 1), :] = recv_h[step, 3, pl.ds(x, 1), :]
            return carry

        lax.fori_loop(0, cx // 8, edges, 0)

    for step in range(STEPS):
        if step % 2 == 0:
            one_step(step, pop_a, pop_b)
        else:
            one_step(step, pop_b, pop_a)
    for step in range(STEPS):
        for n in range(8):
            @pl.when(there(*OFFSETS[n]))
            def _():
                ghost_copy(step, n).wait_send()
        for n in range(4):
            @pl.when(there(*SIDES[n]))
            def _():
                halo_copy(step, n).wait_send()


def store(prof, pop, prof_out, pop_out, sems):
    cx = pop_out.shape[1]
    store_pop = pltpu.make_async_copy(pop.at[:, pl.ds(1, cx)], pop_out, sems.at[0])
    store_prof = pltpu.make_async_copy(prof, prof_out, sems.at[1])
    store_pop.start()
    store_prof.start()
    store_pop.wait()
    store_prof.wait()


def on_device(
    profiles, radial, rate_const, transfer_coef, live_count, send_lists, cell_index, contact_cols,
    contact_blocks, populations,
):
    slots = profiles.shape[1]
    own = slots // BLK
    kb = contact_cols.shape[1]
    _, cx, cy, nz = populations.shape
    rows = cx * cy
    vmem = pl.BlockSpec(memory_space=pltpu.VMEM)
    smem = pl.BlockSpec(memory_space=pltpu.SMEM)
    anywhere = pl.BlockSpec(memory_space=pl.ANY)
    hbm = pl.BlockSpec(memory_space=pltpu.HBM)
    state = pl.pallas_call(
        kernel,
        out_shape=(
            jax.ShapeDtypeStruct(profiles.shape, F32),
            jax.ShapeDtypeStruct((7, cx + 2, cy, nz), F32),
        ),
        in_specs=[smem, smem] + [hbm] * 8,
        out_specs=(vmem, vmem),
        scratch_shapes=[
            pltpu.VMEM((7, cx + 2, cy, nz), F32),
            pltpu.VMEM((own, BLK), F32),
            pltpu.VMEM((own, BLK), F32),
            pltpu.VMEM((own, BLK), jnp.int32),
            pltpu.VMEM((8, BLK), jnp.int32),
            pltpu.VMEM((2, BLK, BLK), F32),
            pltpu.VMEM((own * kb, BLK, BLK), F32),
            pltpu.VMEM((own * kb, BLK, 2 * BLK), BF16),
            pltpu.VMEM((2, 2 * BLK, 2 * BLK), BF16),
            pltpu.VMEM((slots, rows), BF16),
            pltpu.VMEM((rows, slots), BF16),
            pltpu.VMEM((8 * BLK, slots), BF16),
            pltpu.VMEM((slots, nz), F32),
            pltpu.VMEM((slots, BLK), F32),
            pltpu.VMEM((slots, BLK), F32),
            pltpu.VMEM((slots, BLK), BF16),
            pltpu.VMEM((own + 8, 2 * BLK, BLK), BF16),
            pltpu.VMEM((cx, cy, nz), F32),
            pltpu.VMEM((rows, 2 * nz), BF16),
            pltpu.VMEM((slots, BLK), F32),
            pltpu.VMEM((slots, 2 * nz), BF16),
            pltpu.VMEM((slots, BLK), F32),
            pltpu.VMEM((STEPS, 8, SHELL, BLK), F32),
            pltpu.VMEM((STEPS, 8, SHELL, BLK), F32),
            pltpu.VMEM((STEPS, 4, cx, nz), F32),
            pltpu.VMEM((STEPS, 4, cx, nz), F32),
            pltpu.SemaphoreType.DMA((8,)),
            pltpu.SemaphoreType.DMA((STEPS, 8)),
            pltpu.SemaphoreType.DMA((STEPS, 8)),
            pltpu.SemaphoreType.DMA((STEPS, 4)),
            pltpu.SemaphoreType.DMA((STEPS, 4)),
        ],
        compiler_params=pltpu.CompilerParams(
            collective_id=0, has_side_effects=True, vmem_limit_bytes=36 * 1024 * 1024
        ),
    )(
        live_count,
        pltpu.with_memory_space_constraint(contact_cols.T, pltpu.HBM),
        *[
            pltpu.with_memory_space_constraint(operand, pltpu.HBM)
            for operand in (
                rate_const.reshape(own, BLK),
                transfer_coef.reshape(own, BLK),
                cell_index.reshape(own, BLK),
                send_lists,
                radial,
                profiles,
                contact_blocks.reshape(own * kb, BLK, BLK),
                populations,
            )
        ],
    )
    return pl.pallas_call(
        store,
        out_shape=(
            jax.ShapeDtypeStruct(profiles.shape, F32),
            jax.ShapeDtypeStruct(populations.shape, F32),
        ),
        in_specs=[anywhere, anywhere],
        out_specs=(hbm, hbm),
        scratch_shapes=[pltpu.SemaphoreType.DMA((2,))],
        compiler_params=pltpu.CompilerParams(vmem_limit_bytes=1024 * 1024),
    )(*state)


def solution(mesh):
    return jax.shard_map(
        on_device,
        mesh=mesh,
        in_specs=(
            P(None, ("gx", "gy"), None),
            P(),
            P(("gx", "gy")),
            P(("gx", "gy")),
            P(("gx", "gy")),
            P(("gx", "gy"), None),
            P(("gx", "gy")),
            P(("gx", "gy"), None),
            P(("gx", "gy"), None, None, None),
            P(None, "gx", "gy", None),
        ),
        out_specs=(P(None, ("gx", "gy"), None), P(None, "gx", "gy", None)),
        check_vma=False,
    )
```
